512 devices in a mesh: ex: 32 (over z_lo, y, core), feat: 16 (over z_hi, x).
Axes of the slice: x: 4, y: 8, z: 8 (z_hi: 4, z_lo: 2; z = z_hi * 2 + z_lo), core: 2. Of those that a mesh axis runs over, the one named last changes fastest.
Arguments:
- train_grads: bfloat16 [65536, 16384], P('ex', 'feat'), may hold values from -6 to 6
- query_grads: bfloat16 [512, 16384], P('ex', 'feat'), may hold values from -2.390625 to 2.390625
- eigenvalues: float32 [16384], P('feat'), may hold values from 0.009 to 8, as said below
Outputs:
- scores: float32 [65536, 512], P('ex', 'feat')
The draws below stay inside these ranges and needn't reach their ends.
Inputs may be any that keep to these rules, and one draw needn't show every extreme that they name: Positive curvature eigenvalues.
All inputs are finite; a program needn't handle non-finite values.
Results may differ from the reference program's by a relative error of at most 0.0029.
Values may be sent and summed in bfloat16 or wider, within the bound.
A program may use at most 64 MiB of HBM per device.

```python
import jax
import jax.numpy as jnp
from jax import lax

F = 16384
NQ = 512
ROW_DEV = 2048
ROWS = 65536
N_EX = 32


def draw_eigenvalues(key, part):
    key = jax.random.fold_in(key, 7)
    index = jnp.arange(F, dtype=jnp.float32)
    base = 2.0 * jnp.exp(-4.0 * index / F)
    factor = jax.random.uniform(key, (F,), jnp.float32, 0.5, 2.0)
    return (base * factor).astype(jnp.float32)


def with_spikes(result, rng, source, target, shards_of, factor):
    def block_of(position):
        return (jnp.arange(result.shape[position]) // (result.shape[position] // shards_of)).reshape((-1,) + (1,) * (result.ndim - 1 - position))

    near = jax.random.permutation(rng, shards_of)[block_of(target)]
    far = (block_of(target) + shards_of // 2) % shards_of
    return jnp.where((block_of(source) == near) | (block_of(source) == far), factor * result, result)


def block_levels(stream_key, dims, shards, low, largest):
    def one(dim, shards_of):
        steps = jax.random.uniform(jax.random.fold_in(jax.random.fold_in(stream_key, 6), dim), (shards_of,), jnp.float32, low / len(shards), largest / len(shards))
        return jnp.repeat(jnp.exp(steps), dims[dim] // shards_of).reshape((-1,) + (1,) * (len(dims) - dim - 1))

    factor_of = one(*shards[0])
    for cut in shards[1:]:
        factor_of = factor_of * one(*cut)
    return factor_of


def bell_draw(rng, shape, deviation, reach, cuts=(), held_as=jnp.bfloat16):
    factor_of = block_levels(rng, shape, cuts, -0.22, 0.18) if cuts else 1.0
    values = jax.random.normal(rng, shape, jnp.float32) * deviation * factor_of
    return jnp.minimum(jnp.maximum(values, -reach), reach).astype(held_as)


def gaussian_with(rng, dims, deviation, limit, split, heavy, kind=jnp.bfloat16):
    array = deviation * jax.random.normal(rng, dims, jnp.float32)
    if split:
        array = array * block_levels(rng, dims, split, -0.22, 0.18)
    return jnp.clip(with_spikes(array, jax.random.fold_in(rng, 3), *heavy), -limit, limit).astype(kind)


def setup_inputs(seed: int = 0) -> dict:
    key_of = jax.random.split(jax.random.key(seed), 4)
    return {
        "train_grads": bell_draw(key_of[0], (ROWS, F), 1.0, 6.0, ((0, 32), (1, 16))),
        "query_grads": gaussian_with(key_of[1], (NQ, F), 0.3, 2.390625, ((0, 32), (1, 16)), (1, 0, 32, 2.75)),
        "eigenvalues": draw_eigenvalues(jax.random.fold_in(key_of[3], 71), 0),
    }


DAMPING = 0.05
EPSILON = 1e-06

def reference(train_grads, query_grads, eigenvalues):
    inverse = 1.0 / (eigenvalues + DAMPING)
    precond = (query_grads.astype(jnp.float32) * inverse[None, :]).astype(jnp.bfloat16)
    raw = lax.dot_general(train_grads, precond, (((1,), (1,)), ((), ())), preferred_element_type=jnp.float32)
    blocks = train_grads.reshape(N_EX, ROW_DEV, F)

    def row_sums(block):
        return lax.optimization_barrier(jnp.sum(jnp.square(block.astype(jnp.float32)) * inverse[None, :], axis=1))
    selfinf = lax.map(row_sums, blocks).reshape(ROWS)
    return raw * lax.rsqrt(selfinf + EPSILON)[:, None]
```

```python
import jax
import jax.numpy as jnp
from jax import lax
from jax.experimental import pallas as pl
from jax.experimental.pallas import tpu as pltpu
from jax.sharding import PartitionSpec as P

DAMPING = 0.05
EPSILON = 1e-06

MESH = pl.DeviceIdType.MESH
F32, BF16 = jnp.float32, jnp.bfloat16
NT = (((1,), (1,)), ((), ()))

ROWS = 2048
DEPTH = 1024
BLOCK = 16
OWNED = 32
NR = 2
R = ROWS // NR
PIECES = [(0, r) for r in range(NR)] + [(q, r) for r in range(NR) for q in (1, 2, 3)]
N = len(PIECES)
LAG = 2

OFFSETS = (0, 1, -1, 2)


def kernel(
    train_hbm, query, eig, out, train, pre, acc, xs1, xs2, xr1, xr2, zs, zr, own, sb, sr,
    load_sem, ag_send, ag_recv, x1_send, x1_recv, x2_send, x2_recv, z_send, z_recv, s_send, s_recv, far_sem,
):
    ex, feat = lax.axis_index("ex"), lax.axis_index("feat")
    core, y, z_lo = lax.rem(ex, 2), lax.rem(ex // 2, 8), ex // 16
    x, z_hi = lax.rem(feat, 4), feat // 4

    def at(dx=0, dy=0, other_z=0, other_core=0, dz=0):
        there = (lax.rem(z_lo + other_z, 2) * 8 + lax.rem(y + dy + 8, 8)) * 2 + lax.rem(core + other_core, 2)
        return {"ex": there, "feat": lax.rem(z_hi + dz + 4, 4) * 4 + lax.rem(x + dx + 4, 4)}

    barrier = pltpu.get_barrier_semaphore()
    near = [at(dx=1), at(dx=-1), at(dz=1), at(dz=-1), at(other_core=1), at(other_z=1)]
    near += [at(dy=d) for d in (1, -1, 2, -2)]
    for device in near:
        pl.semaphore_signal(barrier, inc=1, device_id=device, device_id_type=MESH)

    loads = []
    for r in range(NR):
        rows = pl.ds(r * R, R)
        load = pltpu.make_async_copy(train_hbm.at[rows], train.at[rows], load_sem.at[r])
        load.start()
        loads.append(load)

    inverse = 1.0 / (eig[...] + DAMPING)

    def slot(quad, place, sibling):
        row = lax.rem(y + OFFSETS[place] + 8, 4) * 32 + lax.rem(core + sibling, 2) * BLOCK
        return pre.at[quad, pl.ds(pl.multiple_of(row, BLOCK), BLOCK)]

    pre[0, pl.ds(pl.multiple_of(lax.rem(y, 4) * 32 + core * BLOCK, BLOCK), BLOCK), :] = (
        query[...].astype(F32) * inverse
    ).astype(BF16)

    sent = []

    def send_block(source, quad, place, sibling, device):
        index = quad * 8 + place * 2 + sibling
        row = lax.rem(y + OFFSETS[source[1]] + 8, 4) * 32 + lax.rem(core + source[2], 2) * BLOCK
        target = pre.at[quad, pl.ds(pl.multiple_of(row, BLOCK), BLOCK)]
        copy = pltpu.make_async_remote_copy(
            src_ref=slot(*source),
            dst_ref=target,
            send_sem=ag_send.at[index],
            recv_sem=ag_recv.at[index],
            device_id=device,
            device_id_type=MESH,
        )
        copy.start()
        sent.append(copy)

    def wait_block(quad, place, sibling):
        index = quad * 8 + place * 2 + sibling
        here = slot(quad, place, sibling)
        pltpu.make_async_remote_copy(
            src_ref=here,
            dst_ref=here,
            send_sem=ag_send.at[index],
            recv_sem=ag_recv.at[index],
            device_id=at(other_core=1),
            device_id_type=MESH,
        ).wait_recv()

    def forward(quad, place):
        wait_block(quad, place, 0)
        send_block((quad, place, 0), quad, place, 1, at(other_core=1))
        if quad == 0:
            send_block((0, place, 0), 1, *{1: (2, 0, at(dy=-2)), 2: (1, 0, at(dy=2)), 3: (0, 0, at(dy=-2))}[place])
        if quad < 2:
            send_block((quad, place, 0), quad + 2, place, 0, at(other_z=1))

    left, right, opposite = lax.rem(x + 3, 4), lax.rem(x + 1, 4), lax.rem(x + 2, 4)
    to_left, to_right = at(dx=-1), at(dx=1)

    def piece_rows(cls, half):
        return pl.ds(pl.multiple_of(cls * 32 + half * 16, 16), 16)

    def x_copy(which, p, side):
        source, target, send, recv = (xs1, xr1, x1_send, x1_recv) if which == 1 else (xs2, xr2, x2_send, x2_recv)
        return pltpu.make_async_remote_copy(
            src_ref=source.at[p, side],
            dst_ref=target.at[p, side],
            send_sem=send.at[p, side],
            recv_sem=recv.at[p, side],
            device_id=(to_left, to_right)[side],
            device_id_type=MESH,
        )

    def multiply(p):
        quad, r = PIECES[p]
        acc[p] = lax.dot_general(pre[quad], train[pl.ds(r * R, R), :], NT, preferred_element_type=F32)
        xs1[p, 0, 0:16] = acc[p, piece_rows(opposite, 0), :].astype(BF16)
        xs1[p, 0, 16:32] = acc[p, piece_rows(left, 1), :].astype(BF16)
        x_copy(1, p, 0).start()
        xs1[p, 1, 0:16] = acc[p, piece_rows(right, 0), :].astype(BF16)
        xs1[p, 1, 16:32] = acc[p, piece_rows(opposite, 1), :].astype(BF16)
        x_copy(1, p, 1).start()

    def relay(p):
        x_copy(1, p, 0).wait_recv()
        xs2[p, 0] = (acc[p, piece_rows(left, 0), :] + xr1[p, 0, 0:16].astype(F32)).astype(BF16)
        x_copy(2, p, 0).start()
        x_copy(1, p, 1).wait_recv()
        xs2[p, 1] = (acc[p, piece_rows(right, 1), :] + xr1[p, 1, 16:32].astype(F32)).astype(BF16)
        x_copy(2, p, 1).start()

    away = lax.rem(x - y + 9, 4) - 1
    bit = lax.rem(y + away + 8, 8) // 4

    def steps_to_owner(quad):
        owner = lax.rem(z_lo + quad // 2, 2) * 2 + lax.rem(bit + quad % 2, 2)
        return lax.rem(z_hi - owner + 4, 4)

    def z_copy(steps, p, r):
        return pltpu.make_async_remote_copy(
            src_ref=zs.at[p],
            dst_ref=zr.at[steps - 1, r],
            send_sem=z_send.at[steps - 1, r],
            recv_sem=z_recv.at[steps - 1, r],
            device_id=at(dz=-steps),
            device_id_type=MESH,
        )

    def collect(p):
        quad, r = PIECES[p]
        x_copy(2, p, 0).wait_recv()
        x_copy(2, p, 1).wait_recv()
        upper = acc[p, piece_rows(x, 0), :] + (xr2[p, 0].astype(F32) + xr1[p, 1, 0:16].astype(F32))
        lower = acc[p, piece_rows(x, 1), :] + (xr1[p, 0, 16:32].astype(F32) + xr2[p, 1].astype(F32))
        steps = steps_to_owner(quad)

        @pl.when(steps == 0)
        def _():
            own[r, 0:16] = upper
            own[r, 16:32] = lower

        @pl.when(steps != 0)
        def _():
            zs[p, 0:16] = upper.astype(BF16)
            zs[p, 16:32] = lower.astype(BF16)
            z_copy(steps, p, r).start()

    def other_x(first):
        there = x + 1 - 2 * lax.rem(x, 2) if first else 3 - x
        return {"ex": ex, "feat": z_hi * 4 + there}

    def other_z_hi(first):
        there = z_hi + 1 - 2 * lax.rem(z_hi, 2) if first else 3 - z_hi
        return {"ex": ex, "feat": there * 4 + x}

    partners = [other_x(True), other_x(False), other_z_hi(True), other_z_hi(False)]

    def self_copy(step):
        return pltpu.make_async_remote_copy(
            src_ref=sb.at[step],
            dst_ref=sr.at[step],
            send_sem=s_send.at[step],
            recv_sem=s_recv.at[step],
            device_id=partners[step],
            device_id_type=MESH,
        )

    def self_step(step):
        self_copy(step).wait_recv()
        sb[step + 1] = sb[step] + sr[step]
        if step < 3:
            self_copy(step + 1).start()

    pl.semaphore_wait(barrier, len(near))
    send_block((0, 0, 0), 0, 1, 0, at(dy=-1))
    send_block((0, 0, 0), 0, 2, 0, at(dy=1))
    send_block((0, 0, 0), 0, 3, 0, at(dy=-2))
    send_block((0, 0, 0), 0, 0, 1, at(other_core=1))
    send_block((0, 0, 0), 1, 3, 0, at(dy=2))
    send_block((0, 0, 0), 2, 0, 0, at(other_z=1))
    pl.semaphore_signal(far_sem, inc=1, device_id=at(dz=1), device_id_type=MESH)

    ones = jnp.ones((8, 128), F32)
    for r in range(NR):
        loads[r].wait()
        wide = train[pl.ds(r * R, R), :].astype(F32)
        squares = wide * wide * inverse
        part = squares[:, 0:128]
        for k in range(1, DEPTH // 128):
            part = part + squares[:, k * 128 : (k + 1) * 128]
        sums = lax.dot_general(ones, part, NT, preferred_element_type=F32, precision=lax.Precision.HIGHEST)
        for k in range(8 // NR):
            sb[0, pl.ds(r * (8 // NR) + k, 1), :] = sums[0:1, k * 256 : (k + 1) * 256]
    self_copy(0).start()

    forward(0, 1)
    forward(0, 2)
    forward(0, 3)
    for place in range(4):
        wait_block(0, place, 1)

    for t in range(N + 2 * LAG):
        if t < N:
            if t == NR:
                for place in (3, 2, 1, 0):
                    forward(1, place)
                for place in range(4):
                    wait_block(1, place, 1)
            elif t == NR + 1:
                for place in range(4):
                    wait_block(2, place, 1)
                for place in (3, 2, 1, 0):
                    forward(3, place)
            elif t == NR + 2:
                for place in range(4):
                    wait_block(3, place, 1)
            multiply(t)
        if t == NR - 1:
            for place in range(4):
                forward(2, place)
        if t == 2 * LAG:
            pl.semaphore_wait(far_sem, 1)
        if 0 <= t - LAG < N:
            relay(t - LAG)
        if 2 <= t < 6:
            self_step(t - 2)
        if t >= 2 * LAG:
            collect(t - 2 * LAG)

    scale = lax.rsqrt(sb[4] + EPSILON)
    for r in range(NR):
        for steps in (1, 2, 3):
            z_copy(steps, 0, r).wait_recv()
        total = own[r] + zr[0, r].astype(F32) + zr[1, r].astype(F32) + zr[2, r].astype(F32)
        for k in range(8 // NR):
            i = r * (8 // NR) + k
            out[:, i * 256 : (i + 1) * 256] = total[:, k * 256 : (k + 1) * 256] * scale[i : i + 1, :]

    for copy in sent:
        copy.wait_send()
    for p in range(N):
        for side in (0, 1):
            x_copy(1, p, side).wait_send()
            x_copy(2, p, side).wait_send()
    for r in range(NR):
        for steps in (1, 2, 3):
            z_copy(steps, 0, r).wait_send()
    for step in range(4):
        self_copy(step).wait_send()


def on_device(train_grads, query_grads, eigenvalues):
    dma = pltpu.SemaphoreType.DMA
    scores = pl.pallas_call(
        kernel,
        out_shape=jax.ShapeDtypeStruct((OWNED, ROWS), F32),
        in_specs=[
            pl.BlockSpec(memory_space=pl.ANY),
            pl.BlockSpec(memory_space=pltpu.VMEM),
            pl.BlockSpec(memory_space=pltpu.VMEM),
        ],
        out_specs=pl.BlockSpec(memory_space=pltpu.VMEM),
        scratch_shapes=[
            pltpu.VMEM((ROWS, DEPTH), BF16),
            pltpu.VMEM((4, 128, DEPTH), BF16),
            pltpu.VMEM((N, 128, R), F32),
            pltpu.VMEM((N, 2, 32, R), BF16),
            pltpu.VMEM((N, 2, 16, R), BF16),
            pltpu.VMEM((N, 2, 32, R), BF16),
            pltpu.VMEM((N, 2, 16, R), BF16),
            pltpu.VMEM((N, OWNED, R), BF16),
            pltpu.VMEM((3, NR, OWNED, R), BF16),
            pltpu.VMEM((NR, OWNED, R), F32),
            pltpu.VMEM((5, 8, 256), F32),
            pltpu.VMEM((4, 8, 256), F32),
            dma((NR,)),
            dma((32,)),
            dma((32,)),
            dma((N, 2)),
            dma((N, 2)),
            dma((N, 2)),
            dma((N, 2)),
            dma((3, NR)),
            dma((3, NR)),
            dma((4,)),
            dma((4,)),
            pltpu.SemaphoreType.REGULAR,
        ],
        compiler_params=pltpu.CompilerParams(
            collective_id=0, has_side_effects=True, vmem_limit_bytes=48 * 2**20
        ),
        cost_estimate=pl.CostEstimate(flops=2 * ROWS * DEPTH * 512, bytes_accessed=6 * 2**20, transcendentals=0),
    )(train_grads, query_grads, eigenvalues.reshape(1, DEPTH))
    return scores.T


def solution(mesh):
    placed = (P("ex", "feat"), P("ex", "feat"), P("feat"))
    return jax.shard_map(
        on_device, mesh=mesh, in_specs=placed, out_specs=P("ex", "feat"), check_vma=False
    )
```

```python
import jax
import jax.numpy as jnp
from jax import lax
from jax.experimental import pallas as pl
from jax.experimental.pallas import tpu as pltpu
from jax.sharding import PartitionSpec as P

DAMPING = 0.05
EPSILON = 1e-06

MESH = pl.DeviceIdType.MESH
F32, BF16 = jnp.float32, jnp.bfloat16
NT = (((1,), (1,)), ((), ()))

ROWS = 2048
DEPTH = 1024
BLOCK = 16
OWNED = 32

OFFSETS = (0, 1, -1, 2)
RUNS = ((0, 512), (512, 1024), (1536, 512))
RELAYED = 1
LONG = RUNS[RELAYED][1]
STRAIGHT = {0: (0, 0), 2: (1, 512)}


def kernel(
    train_hbm, query_hbm, eig_hbm, out, train, query, eig, pre, keep, xs, xr, zs, zr, zkeep, ds, dr, own, sb, sr,
    load_sem, ag_send, ag_recv, x_send, x_recv, z_send, z_recv, d_send, d_recv, s_send, s_recv,
):
    ex, feat = lax.axis_index("ex"), lax.axis_index("feat")
    core, y, z_lo = lax.rem(ex, 2), lax.rem(ex // 2, 8), ex // 16
    x, z_hi = lax.rem(feat, 4), feat // 4

    def at(dx=0, dy=0, other_z=0, other_core=0, dz=0):
        there = (lax.rem(z_lo + other_z, 2) * 8 + lax.rem(y + dy + 8, 8)) * 2 + lax.rem(core + other_core, 2)
        return {"ex": there, "feat": lax.rem(z_hi + dz + 4, 4) * 4 + lax.rem(x + dx + 4, 4)}

    barrier = pltpu.get_barrier_semaphore()
    near = [at(other_core=1), at(other_z=1)] + [at(dy=d) for d in (1, -1, 2, -2)]
    near += [at(dx=1), at(dx=-1)] + [at(dz=d) for d in (1, -1, 2)]
    for device in near:
        pl.semaphore_signal(barrier, inc=1, device_id=device, device_id_type=MESH)

    small = [
        pltpu.make_async_copy(query_hbm, query, load_sem.at[len(RUNS)]),
        pltpu.make_async_copy(eig_hbm, eig, load_sem.at[len(RUNS) + 1]),
    ]
    for load in small:
        load.start()
    loads = []
    for r, run in enumerate(RUNS):
        rows = pl.ds(*run)
        load = pltpu.make_async_copy(train_hbm.at[rows], train.at[rows], load_sem.at[r])
        load.start()
        loads.append(load)
    for load in small:
        load.wait()
    inverse = 1.0 / (eig[...] + DAMPING)

    def slot(quad, place, block_place, sibling):
        role = lax.rem(y + OFFSETS[block_place] - x + 8, 4)
        half = lax.rem(core + sibling, 2) * BLOCK
        return pre.at[quad, pl.ds(pl.multiple_of(role * 32 + half, BLOCK), BLOCK)]

    def block_copy(source, target, device):
        quad, place, sibling = target
        index = quad * 8 + place * 2 + sibling
        return pltpu.make_async_remote_copy(
            src_ref=slot(source[0], source[1], source[1], source[2]),
            dst_ref=slot(quad, place, source[1], source[2]),
            send_sem=ag_send.at[index],
            recv_sem=ag_recv.at[index],
            device_id=device,
            device_id_type=MESH,
        )

    sent = []

    def send_block(source, target, device):
        copy = block_copy(source, target, device)
        copy.start()
        sent.append(copy)

    def wait_block(quad, place, sibling):
        block_copy((quad, place, sibling), (quad, place, sibling), at(other_core=1)).wait_recv()

    beyond = {1: (2, -2), 2: (1, 2), 3: (0, -2)}

    def forward(quad, place):
        wait_block(quad, place, 0)
        here = (quad, place, 0)
        send_block(here, (quad, place, 1), at(other_core=1))
        if quad < 2:
            send_block(here, (quad + 2, place, 0), at(other_z=1))
        if quad == 0:
            further, step = beyond[place]
            send_block(here, (1, further, 0), at(dy=step))

    to_left, to_right = at(dx=-1), at(dx=1)

    def x_copy(quad, r, side, kind):
        rows = pl.ds(*RUNS[r])
        piece = quad * len(RUNS) + r
        return pltpu.make_async_remote_copy(
            src_ref=xs.at[quad, side, kind, :, rows],
            dst_ref=xr.at[quad, side, kind, :, rows],
            send_sem=x_send.at[piece, side, kind],
            recv_sem=x_recv.at[piece, side, kind],
            device_id=(to_left, to_right)[side],
            device_id_type=MESH,
        )

    def multiply(quad, r):
        rows = pl.ds(*RUNS[r])
        product = lax.dot_general(pre[quad], train[rows, :], NT, preferred_element_type=F32)
        xs[quad, 0, 0, :, rows] = product[64:80].astype(BF16)
        xs[quad, 1, 0, :, rows] = product[80:96].astype(BF16)
        x_copy(quad, r, 0, 0).start()
        x_copy(quad, r, 1, 0).start()
        xs[quad, 0, 1, :, rows] = product[112:128].astype(BF16)
        xs[quad, 1, 1, :, rows] = product[32:48].astype(BF16)
        x_copy(quad, r, 0, 1).start()
        x_copy(quad, r, 1, 1).start()
        keep[quad, 0:32, rows] = product[0:32]
        keep[quad, 32:48, rows] = product[96:112]
        keep[quad, 48:64, rows] = product[48:64]

    def relay(quad, r):
        rows = pl.ds(*RUNS[r])
        for side in (0, 1):
            x_copy(quad, r, side, 0).wait_recv()
            mine = keep[quad, 32 + side * 16 : 48 + side * 16, rows]
            xs[quad, side, 2, :, rows] = (mine + xr[quad, side, 0, :, rows].astype(F32)).astype(BF16)
            x_copy(quad, r, side, 2).start()

    bit = lax.rem(y + lax.rem(x - y + 9, 4) - 1 + 8, 8) // 4

    def steps_to_owner(quad):
        owner = lax.rem(z_lo + quad // 2, 2) * 2 + lax.rem(bit + quad % 2, 2)
        return lax.rem(z_hi - owner + 4, 4)

    to_down, to_up = at(dz=-1), at(dz=1)

    def z_copy(kind):
        return pltpu.make_async_remote_copy(
            src_ref=zs.at[kind],
            dst_ref=zr.at[kind],
            send_sem=z_send.at[kind],
            recv_sem=z_recv.at[kind],
            device_id=(to_down, to_up)[kind % 2],
            device_id_type=MESH,
        )

    def direct_copy(steps, r):
        i, start = STRAIGHT[r]
        rows = pl.ds(start, RUNS[r][1])
        return pltpu.make_async_remote_copy(
            src_ref=ds.at[steps - 1, :, rows],
            dst_ref=dr.at[steps - 1, :, rows],
            send_sem=d_send.at[steps - 1, i],
            recv_sem=d_recv.at[steps - 1, i],
            device_id=at(dz=-steps),
            device_id_type=MESH,
        )

    def collect(quad, r):
        start, count = RUNS[r]
        rows = pl.ds(start, count)
        for side in (0, 1):
            x_copy(quad, r, side, 1).wait_recv()
            x_copy(quad, r, side, 2).wait_recv()
        got = lambda side, kind: xr[quad, side, kind, :, rows].astype(F32)
        upper = keep[quad, 0:16, rows] + (got(0, 2) + got(1, 1))
        lower = keep[quad, 16:32, rows] + (got(0, 1) + got(1, 2))
        steps = steps_to_owner(quad)

        @pl.when(steps == 0)
        def _():
            own[0:16, rows] = upper
            own[16:32, rows] = lower

        if r != RELAYED:

            @pl.when(steps != 0)
            def _():
                ds[steps - 1, 0:16, pl.ds(STRAIGHT[r][1], count)] = upper.astype(BF16)
                ds[steps - 1, 16:32, pl.ds(STRAIGHT[r][1], count)] = lower.astype(BF16)
                direct_copy(steps, r).start()

            return

        @pl.when(steps == 2)
        def _():
            zs[0] = upper.astype(BF16)
            zs[1] = lower.astype(BF16)
            z_copy(0).start()
            z_copy(1).start()

        @pl.when(steps == 1)
        def _():
            zs[2] = lower.astype(BF16)
            z_copy(2).start()
            zkeep[0] = upper

        @pl.when(steps == 3)
        def _():
            zs[3] = upper.astype(BF16)
            z_copy(3).start()
            zkeep[1] = lower

    def z_relay():
        for side in (0, 1):
            z_copy(side).wait_recv()
            zs[4 + side] = (zkeep[side] + zr[side].astype(F32)).astype(BF16)
            z_copy(4 + side).start()

    def finish(r, scale):
        start, count = RUNS[r]
        rows = pl.ds(start, count)
        if r == RELAYED:
            for kind in (2, 3, 4, 5):
                z_copy(kind).wait_recv()
            upper = own[0:16, rows] + (zr[4].astype(F32) + zr[3].astype(F32))
            lower = own[16:32, rows] + (zr[2].astype(F32) + zr[5].astype(F32))
        else:
            for steps in (1, 2, 3):
                direct_copy(steps, r).wait_recv()
            parts = dr[:, :, pl.ds(STRAIGHT[r][1], count)].astype(F32)
            total = own[:, rows] + (parts[0] + parts[1] + parts[2])
            upper, lower = total[0:16], total[16:32]
        for k in range(count // 256):
            i = start // 256 + k
            columns = slice(k * 256, (k + 1) * 256)
            out[0:16, i * 256 : (i + 1) * 256] = upper[:, columns] * scale[i : i + 1, :]
            out[16:32, i * 256 : (i + 1) * 256] = lower[:, columns] * scale[i : i + 1, :]

    def partner(step):
        pair = lambda i: i + 1 - 2 * lax.rem(i, 2)
        if step < 2:
            return {"ex": ex, "feat": z_hi * 4 + (pair(x) if step == 0 else 3 - x)}
        return {"ex": ex, "feat": (pair(z_hi) if step == 2 else 3 - z_hi) * 4 + x}

    def self_copy(step):
        return pltpu.make_async_remote_copy(
            src_ref=sb.at[step],
            dst_ref=sr.at[step],
            send_sem=s_send.at[step],
            recv_sem=s_recv.at[step],
            device_id=partner(step),
            device_id_type=MESH,
        )

    def self_step(step):
        self_copy(step).wait_recv()
        sb[step + 1] = sb[step] + sr[step]
        if step < 3:
            self_copy(step + 1).start()

    mine = lax.rem(y - x + 8, 4) * 32 + core * BLOCK
    pre[0, pl.ds(pl.multiple_of(mine, BLOCK), BLOCK), :] = (query[...].astype(F32) * inverse).astype(BF16)

    ones = jnp.ones((8, 128), F32)

    def self_influence(r):
        start, count = RUNS[r]
        loads[r].wait()
        wide = train[pl.ds(start, count), :].astype(F32)
        squares = wide * wide * inverse
        part = squares[:, 0:128]
        for k in range(1, DEPTH // 128):
            part = part + squares[:, k * 128 : (k + 1) * 128]
        sums = lax.dot_general(ones, part, NT, preferred_element_type=F32, precision=lax.Precision.HIGHEST)
        for k in range(count // 256):
            sb[0, pl.ds(start // 256 + k, 1), :] = sums[0:1, k * 256 : (k + 1) * 256]

    pl.semaphore_wait(barrier, len(near))
    here = (0, 0, 0)
    send_block(here, (0, 1, 0), at(dy=-1))
    send_block(here, (0, 2, 0), at(dy=1))
    send_block(here, (0, 3, 0), at(dy=-2))
    send_block(here, (0, 0, 1), at(other_core=1))
    send_block(here, (2, 0, 0), at(other_z=1))
    send_block(here, (1, 3, 0), at(dy=2))
    for r in range(len(RUNS)):
        self_influence(r)
    self_copy(0).start()

    for place in (1, 2, 3):
        forward(0, place)
    for place in (0, 1, 2, 3):
        wait_block(0, place, 1)
    multiply(0, 0)
    forward(2, 0)
    multiply(0, 1)
    forward(1, 3)
    multiply(0, 2)
    for place in (1, 2, 3):
        forward(2, place)
    self_step(0)
    for place in (0, 1, 2, 3):
        wait_block(2, place, 1)
    multiply(2, 0)
    for place in (2, 1, 0):
        forward(1, place)
    relay(0, 0)
    multiply(2, 1)
    relay(0, 1)
    multiply(2, 2)
    relay(0, 2)
    for place in (0, 1, 2, 3):
        wait_block(1, place, 1)
    multiply(1, 0)
    self_step(1)
    relay(2, 0)
    for place in (3, 2, 1, 0):
        forward(3, place)
    collect(0, 0)
    relay(2, 1)
    relay(2, 2)
    for place in (0, 1, 2, 3):
        wait_block(3, place, 1)
    multiply(3, 0)
    multiply(1, 1)
    collect(0, 1)
    collect(0, 2)
    relay(1, 0)
    multiply(3, 1)
    multiply(1, 2)
    multiply(3, 2)
    collect(2, 0)
    relay(3, 0)
    relay(1, 1)
    self_step(2)
    collect(2, 1)
    collect(2, 2)
    relay(3, 1)
    collect(1, 0)
    relay(1, 2)
    relay(3, 2)
    collect(3, 0)
    self_step(3)
    scale = lax.rsqrt(sb[4] + EPSILON)
    collect(1, 1)
    collect(3, 1)
    collect(1, 2)
    collect(3, 2)
    z_relay()
    finish(0, scale)
    finish(1, scale)
    finish(2, scale)

    for copy in sent:
        copy.wait_send()
    for quad in range(4):
        for r in range(len(RUNS)):
            for side in (0, 1):
                for kind in range(3):
                    x_copy(quad, r, side, kind).wait_send()
    for kind in range(6):
        z_copy(kind).wait_send()
    for steps in (1, 2, 3):
        for r in STRAIGHT:
            direct_copy(steps, r).wait_send()
    for step in range(4):
        self_copy(step).wait_send()


def on_device(train_grads, query_grads, eigenvalues):
    dma = pltpu.SemaphoreType.DMA
    scores = pl.pallas_call(
        kernel,
        out_shape=pltpu.VMEM((OWNED, ROWS), F32),
        in_specs=[pl.BlockSpec(memory_space=pltpu.HBM)] * 3,
        out_specs=pl.BlockSpec(memory_space=pltpu.VMEM),
        scratch_shapes=[
            pltpu.VMEM((ROWS, DEPTH), BF16),
            pltpu.VMEM((BLOCK, DEPTH), BF16),
            pltpu.VMEM((1, DEPTH), F32),
            pltpu.VMEM((4, 128, DEPTH), BF16),
            pltpu.VMEM((4, 64, ROWS), F32),
            pltpu.VMEM((4, 2, 3, 16, ROWS), BF16),
            pltpu.VMEM((4, 2, 3, 16, ROWS), BF16),
            pltpu.VMEM((6, 16, LONG), BF16),
            pltpu.VMEM((6, 16, LONG), BF16),
            pltpu.VMEM((2, 16, LONG), F32),
            pltpu.VMEM((3, OWNED, ROWS - LONG), BF16),
            pltpu.VMEM((3, OWNED, ROWS - LONG), BF16),
            pltpu.VMEM((OWNED, ROWS), F32),
            pltpu.VMEM((5, 8, 256), F32),
            pltpu.VMEM((4, 8, 256), F32),
            dma((len(RUNS) + 2,)),
            dma((32,)),
            dma((32,)),
            dma((4 * len(RUNS), 2, 3)),
            dma((4 * len(RUNS), 2, 3)),
            dma((6,)),
            dma((6,)),
            dma((3, len(STRAIGHT))),
            dma((3, len(STRAIGHT))),
            dma((4,)),
            dma((4,)),
        ],
        compiler_params=pltpu.CompilerParams(
            collective_id=0, has_side_effects=True, vmem_limit_bytes=60 * 2**20
        ),
        cost_estimate=pl.CostEstimate(flops=2 * ROWS * DEPTH * 512, bytes_accessed=6 * 2**20, transcendentals=0),
    )(train_grads, query_grads, eigenvalues.reshape(1, DEPTH))
    return scores.T


def solution(mesh):
    placed = (P("ex", "feat"), P("ex", "feat"), P("feat"))
    return jax.shard_map(
        on_device, mesh=mesh, in_specs=placed, out_specs=P("ex", "feat"), check_vma=False
    )
```

```python
import jax
import jax.numpy as jnp
from jax import lax
from jax.experimental import pallas as pl
from jax.experimental.pallas import tpu as pltpu
from jax.sharding import PartitionSpec as P

DAMPING = 0.05
EPSILON = 1e-06

MESH = pl.DeviceIdType.MESH
F32, BF16 = jnp.float32, jnp.bfloat16
NT = (((1,), (1,)), ((), ()))

ROWS = 2048
DEPTH = 1024
BLOCK = 16
OWNED = 32

OFFSETS = (0, 1, -1, 2)
RUNS = ((0, 768), (768, 768), (1536, 512))
RELAYED = 1
LONG = RUNS[RELAYED][1]
STRAIGHT = {0: (0, 0), 2: (1, 768)}


def kernel(
    train_hbm, query_hbm, eig_hbm, out, train, query, eig, pre, keep, xs, xr, zs, zr, zkeep, ds, dr, own, sb, sr,
    load_sem, ag_send, ag_recv, x_send, x_recv, z_send, z_recv, d_send, d_recv, s_send, s_recv,
):
    ex, feat = lax.axis_index("ex"), lax.axis_index("feat")
    core, y, z_lo = lax.rem(ex, 2), lax.rem(ex // 2, 8), ex // 16
    x, z_hi = lax.rem(feat, 4), feat // 4

    def at(dx=0, dy=0, other_z=0, other_core=0, dz=0):
        there = (lax.rem(z_lo + other_z, 2) * 8 + lax.rem(y + dy + 8, 8)) * 2 + lax.rem(core + other_core, 2)
        return {"ex": there, "feat": lax.rem(z_hi + dz + 4, 4) * 4 + lax.rem(x + dx + 4, 4)}

    barrier = pltpu.get_barrier_semaphore()
    near = [at(other_core=1), at(other_z=1)] + [at(dy=d) for d in (1, -1, 2, -2)]
    near += [at(dx=1), at(dx=-1)] + [at(dz=d) for d in (1, -1, 2)]
    for device in near:
        pl.semaphore_signal(barrier, inc=1, device_id=device, device_id_type=MESH)

    small = [
        pltpu.make_async_copy(query_hbm, query, load_sem.at[len(RUNS)]),
        pltpu.make_async_copy(eig_hbm, eig, load_sem.at[len(RUNS) + 1]),
    ]
    for load in small:
        load.start()
    loads = []
    for r, run in enumerate(RUNS):
        rows = pl.ds(*run)
        load = pltpu.make_async_copy(train_hbm.at[rows], train.at[rows], load_sem.at[r])
        load.start()
        loads.append(load)
    for load in small:
        load.wait()
    inverse = 1.0 / (eig[...] + DAMPING)

    def slot(quad, place, block_place, sibling):
        role = lax.rem(y + OFFSETS[block_place] - x + 8, 4)
        half = lax.rem(core + sibling, 2) * BLOCK
        return pre.at[quad, pl.ds(pl.multiple_of(role * 32 + half, BLOCK), BLOCK)]

    def block_copy(source, target, device):
        quad, place, sibling = target
        index = quad * 8 + place * 2 + sibling
        return pltpu.make_async_remote_copy(
            src_ref=slot(source[0], source[1], source[1], source[2]),
            dst_ref=slot(quad, place, source[1], source[2]),
            send_sem=ag_send.at[index],
            recv_sem=ag_recv.at[index],
            device_id=device,
            device_id_type=MESH,
        )

    sent = []

    def send_block(source, target, device):
        copy = block_copy(source, target, device)
        copy.start()
        sent.append(copy)

    def wait_block(quad, place, sibling):
        block_copy((quad, place, sibling), (quad, place, sibling), at(other_core=1)).wait_recv()

    beyond = {0: (3, 2), 1: (2, -2), 2: (1, 2), 3: (0, -2)}

    def forward(quad, place):
        wait_block(quad, place, 0)
        here = (quad, place, 0)
        send_block(here, (quad, place, 1), at(other_core=1))
        if quad == 0:
            send_block(here, (quad + 2, place, 0), at(other_z=1))
        if quad in (0, 2):
            further, step = beyond[place]
            send_block(here, (quad + 1, further, 0), at(dy=step))

    to_left, to_right = at(dx=-1), at(dx=1)

    def x_copy(quad, r, side, kind):
        rows = pl.ds(*RUNS[r])
        piece = quad * len(RUNS) + r
        return pltpu.make_async_remote_copy(
            src_ref=xs.at[quad, side, kind, :, rows],
            dst_ref=xr.at[quad, side, kind, :, rows],
            send_sem=x_send.at[piece, side, kind],
            recv_sem=x_recv.at[piece, side, kind],
            device_id=(to_left, to_right)[side],
            device_id_type=MESH,
        )

    def multiply(quad, r):
        rows = pl.ds(*RUNS[r])
        product = lax.dot_general(pre[quad], train[rows, :], NT, preferred_element_type=F32)
        xs[quad, 0, 0, :, rows] = product[64:80].astype(BF16)
        xs[quad, 1, 0, :, rows] = product[80:96].astype(BF16)
        x_copy(quad, r, 0, 0).start()
        x_copy(quad, r, 1, 0).start()
        xs[quad, 0, 1, :, rows] = product[112:128].astype(BF16)
        xs[quad, 1, 1, :, rows] = product[32:48].astype(BF16)
        if not (quad != 0):
            x_copy(quad, r, 0, 1).start()
            x_copy(quad, r, 1, 1).start()
        keep[quad, 0:32, rows] = product[0:32]
        keep[quad, 32:48, rows] = product[96:112]
        keep[quad, 48:64, rows] = product[48:64]

    def multiply_half(other):
        half = lax.rem(core + other, 2)
        rows = pl.ds(*RUNS[0])
        roles = (0, 2, 1 + 2 * half, 3 - 2 * half)
        queries = [pre[0, pl.ds(pl.multiple_of(role * 32 + half * 16, 16), 16), :] for role in roles]
        product = lax.dot_general(jnp.concatenate(queries), train[rows, :], NT, preferred_element_type=F32)

        def send(side, kind, value):
            xs[0, side, kind, :, rows] = value.astype(BF16)
            pltpu.make_async_remote_copy(
                src_ref=xs.at[0, side, kind, :, rows],
                dst_ref=xr.at[0, side, kind, :, rows],
                send_sem=x_send.at[0, side, kind],
                recv_sem=x_recv.at[0, side, kind],
                device_id=at(dx=2 * side - 1),
                device_id_type=MESH,
            ).start()

        send(half, 0, product[16:32])
        send(1 - half, 1, product[32:48])
        keep[0, pl.ds(pl.multiple_of(half * 16, 16), 16), rows] = product[0:16]
        keep[0, pl.ds(pl.multiple_of(32 + half * 16, 16), 16), rows] = product[48:64]

    def relay(quad, r):
        rows = pl.ds(*RUNS[r])
        if quad != 0:
            x_copy(quad, r, 0, 1).start()
            x_copy(quad, r, 1, 1).start()
        for side in (0, 1):
            x_copy(quad, r, side, 0).wait_recv()
            mine = keep[quad, 32 + side * 16 : 48 + side * 16, rows]
            xs[quad, side, 2, :, rows] = (mine + xr[quad, side, 0, :, rows].astype(F32)).astype(BF16)
            x_copy(quad, r, side, 2).start()

    bit = lax.rem(y + lax.rem(x - y + 9, 4) - 1 + 8, 8) // 4

    def steps_to_owner(quad):
        owner = lax.rem(z_lo + quad // 2, 2) * 2 + lax.rem(bit + quad % 2, 2)
        return lax.rem(z_hi - owner + 4, 4)

    to_down, to_up = at(dz=-1), at(dz=1)

    def z_copy(kind):
        return pltpu.make_async_remote_copy(
            src_ref=zs.at[kind],
            dst_ref=zr.at[kind],
            send_sem=z_send.at[kind],
            recv_sem=z_recv.at[kind],
            device_id=(to_down, to_up)[kind % 2],
            device_id_type=MESH,
        )

    def direct_copy(steps, r):
        i, start = STRAIGHT[r]
        rows = pl.ds(start, RUNS[r][1])
        return pltpu.make_async_remote_copy(
            src_ref=ds.at[steps - 1, :, rows],
            dst_ref=dr.at[steps - 1, :, rows],
            send_sem=d_send.at[steps - 1, i],
            recv_sem=d_recv.at[steps - 1, i],
            device_id=at(dz=-steps),
            device_id_type=MESH,
        )

    def collect(quad, r):
        start, count = RUNS[r]
        rows = pl.ds(start, count)
        for side in (0, 1):
            x_copy(quad, r, side, 1).wait_recv()
            x_copy(quad, r, side, 2).wait_recv()
        got = lambda side, kind: xr[quad, side, kind, :, rows].astype(F32)
        upper = keep[quad, 0:16, rows] + (got(0, 2) + got(1, 1))
        lower = keep[quad, 16:32, rows] + (got(0, 1) + got(1, 2))
        steps = steps_to_owner(quad)

        @pl.when(steps == 0)
        def _():
            own[0:16, rows] = upper
            own[16:32, rows] = lower

        if r != RELAYED:

            @pl.when(steps != 0)
            def _():
                ds[steps - 1, 0:16, pl.ds(STRAIGHT[r][1], count)] = upper.astype(BF16)
                ds[steps - 1, 16:32, pl.ds(STRAIGHT[r][1], count)] = lower.astype(BF16)
                direct_copy(steps, r).start()

            return

        @pl.when(steps == 2)
        def _():
            zs[0] = upper.astype(BF16)
            zs[1] = lower.astype(BF16)
            z_copy(0).start()
            z_copy(1).start()

        @pl.when(steps == 1)
        def _():
            zs[2] = lower.astype(BF16)
            z_copy(2).start()
            zkeep[0] = upper

        @pl.when(steps == 3)
        def _():
            zs[3] = upper.astype(BF16)
            z_copy(3).start()
            zkeep[1] = lower

    def z_relay():
        for side in (0, 1):
            z_copy(side).wait_recv()
            zs[4 + side] = (zkeep[side] + zr[side].astype(F32)).astype(BF16)
            z_copy(4 + side).start()

    def finish(r, scale):
        start, count = RUNS[r]
        rows = pl.ds(start, count)
        if r == RELAYED:
            for kind in (2, 3, 4, 5):
                z_copy(kind).wait_recv()
            upper = own[0:16, rows] + (zr[4].astype(F32) + zr[3].astype(F32))
            lower = own[16:32, rows] + (zr[2].astype(F32) + zr[5].astype(F32))
        else:
            for steps in (1, 2, 3):
                direct_copy(steps, r).wait_recv()
            parts = dr[:, :, pl.ds(STRAIGHT[r][1], count)].astype(F32)
            total = own[:, rows] + (parts[0] + parts[1] + parts[2])
            upper, lower = total[0:16], total[16:32]
        for k in range(count // 256):
            i = start // 256 + k
            columns = slice(k * 256, (k + 1) * 256)
            out[0:16, i * 256 : (i + 1) * 256] = upper[:, columns] * scale[i : i + 1, :]
            out[16:32, i * 256 : (i + 1) * 256] = lower[:, columns] * scale[i : i + 1, :]

    def partner(step):
        pair = lambda i: i + 1 - 2 * lax.rem(i, 2)
        if step < 2:
            return {"ex": ex, "feat": z_hi * 4 + (pair(x) if step == 0 else 3 - x)}
        return {"ex": ex, "feat": (pair(z_hi) if step == 2 else 3 - z_hi) * 4 + x}

    def self_copy(step):
        return pltpu.make_async_remote_copy(
            src_ref=sb.at[step],
            dst_ref=sr.at[step],
            send_sem=s_send.at[step],
            recv_sem=s_recv.at[step],
            device_id=partner(step),
            device_id_type=MESH,
        )

    def self_step(step):
        self_copy(step).wait_recv()
        sb[step + 1] = sb[step] + sr[step]
        if step < 3:
            self_copy(step + 1).start()

    mine = lax.rem(y - x + 8, 4) * 32 + core * BLOCK
    pre[0, pl.ds(pl.multiple_of(mine, BLOCK), BLOCK), :] = (query[...].astype(F32) * inverse).astype(BF16)

    ones = jnp.ones((8, 128), F32)

    def self_influence(r):
        start, count = RUNS[r]
        loads[r].wait()
        wide = train[pl.ds(start, count), :].astype(F32)
        squares = wide * wide * inverse
        part = squares[:, 0:128]
        for k in range(1, DEPTH // 128):
            part = part + squares[:, k * 128 : (k + 1) * 128]
        sums = lax.dot_general(ones, part, NT, preferred_element_type=F32, precision=lax.Precision.HIGHEST)
        for k in range(count // 256):
            sb[0, pl.ds(start // 256 + k, 1), :] = sums[0:1, k * 256 : (k + 1) * 256]

    pl.semaphore_wait(barrier, len(near))
    here = (0, 0, 0)
    send_block(here, (0, 1, 0), at(dy=-1))
    send_block(here, (0, 2, 0), at(dy=1))
    send_block(here, (0, 3, 0), at(dy=-2))
    send_block(here, (0, 0, 1), at(other_core=1))
    self_influence(0)
    send_block(here, (2, 0, 0), at(other_z=1))
    send_block(here, (1, 3, 0), at(dy=2))
    self_influence(1)
    self_influence(2)
    self_copy(0).start()

    for place in (1, 2, 3):
        forward(0, place)
    multiply_half(0)
    for place in (0, 1, 2, 3):
        wait_block(0, place, 1)
    multiply_half(1)
    forward(2, 0)
    multiply(0, 1)
    forward(1, 3)
    multiply(0, 2)
    for place in (1, 2, 3):
        forward(2, place)
    self_step(0)
    for place in (0, 1, 2, 3):
        wait_block(2, place, 1)
    multiply(2, 0)
    for place in (2, 1, 0):
        forward(1, place)
    relay(0, 0)
    multiply(2, 1)
    relay(0, 1)
    multiply(2, 2)
    relay(0, 2)
    for place in (0, 1, 2, 3):
        wait_block(1, place, 1)
    multiply(1, 0)
    self_step(1)
    relay(2, 0)
    for place in (3, 2, 1, 0):
        forward(3, place)
    collect(0, 0)
    relay(2, 1)
    relay(2, 2)
    for place in (0, 1, 2, 3):
        wait_block(3, place, 1)
    multiply(3, 0)
    multiply(1, 1)
    collect(0, 1)
    collect(0, 2)
    relay(1, 0)
    multiply(3, 1)
    multiply(1, 2)
    multiply(3, 2)
    collect(2, 0)
    relay(3, 0)
    relay(1, 1)
    self_step(2)
    collect(2, 1)
    collect(2, 2)
    relay(3, 1)
    collect(1, 0)
    relay(1, 2)
    relay(3, 2)
    collect(3, 0)
    self_step(3)
    scale = lax.rsqrt(sb[4] + EPSILON)
    collect(1, 1)
    collect(3, 1)
    collect(1, 2)
    collect(3, 2)
    z_relay()
    finish(0, scale)
    finish(1, scale)
    finish(2, scale)

    for copy in sent:
        copy.wait_send()
    for quad in range(4):
        for r in range(len(RUNS)):
            for side in (0, 1):
                for kind in range(3):
                    x_copy(quad, r, side, kind).wait_send()
    for kind in range(6):
        z_copy(kind).wait_send()
    for steps in (1, 2, 3):
        for r in STRAIGHT:
            direct_copy(steps, r).wait_send()
    for step in range(4):
        self_copy(step).wait_send()


def on_device(train_grads, query_grads, eigenvalues):
    dma = pltpu.SemaphoreType.DMA
    scores = pl.pallas_call(
        kernel,
        out_shape=pltpu.VMEM((OWNED, ROWS), F32),
        in_specs=[pl.BlockSpec(memory_space=pltpu.HBM)] * 3,
        out_specs=pl.BlockSpec(memory_space=pltpu.VMEM),
        scratch_shapes=[
            pltpu.VMEM((ROWS, DEPTH), BF16),
            pltpu.VMEM((BLOCK, DEPTH), BF16),
            pltpu.VMEM((1, DEPTH), F32),
            pltpu.VMEM((4, 128, DEPTH), BF16),
            pltpu.VMEM((4, 64, ROWS), F32),
            pltpu.VMEM((4, 2, 3, 16, ROWS), BF16),
            pltpu.VMEM((4, 2, 3, 16, ROWS), BF16),
            pltpu.VMEM((6, 16, LONG), BF16),
            pltpu.VMEM((6, 16, LONG), BF16),
            pltpu.VMEM((2, 16, LONG), F32),
            pltpu.VMEM((3, OWNED, ROWS - LONG), BF16),
            pltpu.VMEM((3, OWNED, ROWS - LONG), BF16),
            pltpu.VMEM((OWNED, ROWS), F32),
            pltpu.VMEM((5, 8, 256), F32),
            pltpu.VMEM((4, 8, 256), F32),
            dma((len(RUNS) + 2,)),
            dma((32,)),
            dma((32,)),
            dma((4 * len(RUNS), 2, 3)),
            dma((4 * len(RUNS), 2, 3)),
            dma((6,)),
            dma((6,)),
            dma((3, len(STRAIGHT))),
            dma((3, len(STRAIGHT))),
            dma((4,)),
            dma((4,)),
        ],
        compiler_params=pltpu.CompilerParams(
            collective_id=0, has_side_effects=True, vmem_limit_bytes=60 * 2**20
        ),
        cost_estimate=pl.CostEstimate(flops=2 * ROWS * DEPTH * 512, bytes_accessed=6 * 2**20, transcendentals=0),
    )(train_grads, query_grads, eigenvalues.reshape(1, DEPTH))
    return scores.T


def solution(mesh):
    placed = (P("ex", "feat"), P("ex", "feat"), P("feat"))
    return jax.shard_map(
        on_device, mesh=mesh, in_specs=placed, out_specs=P("ex", "feat"), check_vma=False
    )
```

```python
import jax
import jax.numpy as jnp
from jax import lax
from jax.experimental import pallas as pl
from jax.experimental.pallas import tpu as pltpu
from jax.sharding import PartitionSpec as P

DAMPING = 0.05
EPSILON = 1e-06

MESH = pl.DeviceIdType.MESH
F32, BF16 = jnp.float32, jnp.bfloat16
NT = (((1,), (1,)), ((), ()))

ROWS = 2048
DEPTH = 1024
BLOCK = 16
OWNED = 32

OFFSETS = (0, 1, -1, 2)
RUNS = ((0, 768), (768, 768), (1536, 512))
RELAYED = 1
LONG = RUNS[RELAYED][1]
STRAIGHT = {0: (0, 0), 2: (1, 768)}


def kernel(
    train_hbm, query_hbm, eig_hbm, out, train, query, eig, pre, keep, xs, xr, zs, zr, zkeep, ds, dr, own, sb, sr,
    load_sem, ag_send, ag_recv, x_send, x_recv, z_send, z_recv, d_send, d_recv, s_send, s_recv,
):
    ex, feat = lax.axis_index("ex"), lax.axis_index("feat")
    core, y, z_lo = lax.rem(ex, 2), lax.rem(ex // 2, 8), ex // 16
    x, z_hi = lax.rem(feat, 4), feat // 4

    def at(dx=0, dy=0, other_z=0, other_core=0, dz=0):
        there = (lax.rem(z_lo + other_z, 2) * 8 + lax.rem(y + dy + 8, 8)) * 2 + lax.rem(core + other_core, 2)
        return {"ex": there, "feat": lax.rem(z_hi + dz + 4, 4) * 4 + lax.rem(x + dx + 4, 4)}

    barrier = pltpu.get_barrier_semaphore()
    near = [at(other_core=1), at(other_z=1)] + [at(dy=d) for d in (1, -1, 2, -2)]
    near += [at(dx=1), at(dx=-1)] + [at(dz=d) for d in (1, -1, 2)]
    for device in near:
        pl.semaphore_signal(barrier, inc=1, device_id=device, device_id_type=MESH)

    small = [
        pltpu.make_async_copy(query_hbm, query, load_sem.at[len(RUNS)]),
        pltpu.make_async_copy(eig_hbm, eig, load_sem.at[len(RUNS) + 1]),
    ]
    for load in small:
        load.start()
    loads = []
    for r, run in enumerate(RUNS):
        rows = pl.ds(*run)
        load = pltpu.make_async_copy(train_hbm.at[rows], train.at[rows], load_sem.at[r])
        load.start()
        loads.append(load)
    for load in small:
        load.wait()
    inverse = 1.0 / (eig[...] + DAMPING)

    def slot(quad, place, block_place, sibling):
        role = lax.rem(y + OFFSETS[block_place] - x + 8, 4)
        half = lax.rem(core + sibling, 2) * BLOCK
        return pre.at[quad, pl.ds(pl.multiple_of(role * 32 + half, BLOCK), BLOCK)]

    def block_copy(source, target, device):
        quad, place, sibling = target
        index = quad * 8 + place * 2 + sibling
        return pltpu.make_async_remote_copy(
            src_ref=slot(source[0], source[1], source[1], source[2]),
            dst_ref=slot(quad, place, source[1], source[2]),
            send_sem=ag_send.at[index],
            recv_sem=ag_recv.at[index],
            device_id=device,
            device_id_type=MESH,
        )

    sent = []

    def send_block(source, target, device):
        copy = block_copy(source, target, device)
        copy.start()
        sent.append(copy)

    def wait_block(quad, place, sibling):
        block_copy((quad, place, sibling), (quad, place, sibling), at(other_core=1)).wait_recv()

    beyond = {0: (3, 2), 1: (2, -2), 2: (1, 2), 3: (0, -2)}

    def forward(quad, place):
        wait_block(quad, place, 0)
        here = (quad, place, 0)
        send_block(here, (quad, place, 1), at(other_core=1))
        if quad == 0:
            send_block(here, (quad + 2, place, 0), at(other_z=1))
        if quad in (0, 2):
            further, step = beyond[place]
            send_block(here, (quad + 1, further, 0), at(dy=step))

    to_left, to_right = at(dx=-1), at(dx=1)

    def x_copy(quad, r, side, kind):
        rows = pl.ds(*RUNS[r])
        piece = quad * len(RUNS) + r
        return pltpu.make_async_remote_copy(
            src_ref=xs.at[quad, side, kind, :, rows],
            dst_ref=xr.at[quad, side, kind, :, rows],
            send_sem=x_send.at[piece, side, kind],
            recv_sem=x_recv.at[piece, side, kind],
            device_id=(to_left, to_right)[side],
            device_id_type=MESH,
        )

    def multiply(quad, r):
        rows = pl.ds(*RUNS[r])
        product = lax.dot_general(pre[quad], train[rows, :], NT, preferred_element_type=F32)
        xs[quad, 0, 0, :, rows] = product[64:80].astype(BF16)
        xs[quad, 1, 0, :, rows] = product[80:96].astype(BF16)
        x_copy(quad, r, 0, 0).start()
        x_copy(quad, r, 1, 0).start()
        xs[quad, 0, 1, :, rows] = product[112:128].astype(BF16)
        xs[quad, 1, 1, :, rows] = product[32:48].astype(BF16)
        if not (quad != 0):
            x_copy(quad, r, 0, 1).start()
            x_copy(quad, r, 1, 1).start()
        keep[quad, 0:32, rows] = product[0:32]
        keep[quad, 32:48, rows] = product[96:112]
        keep[quad, 48:64, rows] = product[48:64]

    def multiply_half(other):
        half = lax.rem(core + other, 2)
        rows = pl.ds(*RUNS[0])
        roles = (0, 2, 1 + 2 * half, 3 - 2 * half)
        queries = [pre[0, pl.ds(pl.multiple_of(role * 32 + half * 16, 16), 16), :] for role in roles]
        product = lax.dot_general(jnp.concatenate(queries), train[rows, :], NT, preferred_element_type=F32)

        def send(side, kind, value):
            xs[0, side, kind, :, rows] = value.astype(BF16)
            pltpu.make_async_remote_copy(
                src_ref=xs.at[0, side, kind, :, rows],
                dst_ref=xr.at[0, side, kind, :, rows],
                send_sem=x_send.at[0, side, kind],
                recv_sem=x_recv.at[0, side, kind],
                device_id=at(dx=2 * side - 1),
                device_id_type=MESH,
            ).start()

        send(half, 0, product[16:32])
        send(1 - half, 1, product[32:48])
        keep[0, pl.ds(pl.multiple_of(half * 16, 16), 16), rows] = product[0:16]
        keep[0, pl.ds(pl.multiple_of(32 + half * 16, 16), 16), rows] = product[48:64]

    def relay(quad, r):
        rows = pl.ds(*RUNS[r])
        if quad != 0:
            x_copy(quad, r, 0, 1).start()
            x_copy(quad, r, 1, 1).start()
        for side in (0, 1):
            x_copy(quad, r, side, 0).wait_recv()
            mine = keep[quad, 32 + side * 16 : 48 + side * 16, rows]
            xs[quad, side, 2, :, rows] = (mine + xr[quad, side, 0, :, rows].astype(F32)).astype(BF16)
            x_copy(quad, r, side, 2).start()

    bit = lax.rem(y + lax.rem(x - y + 9, 4) - 1 + 8, 8) // 4

    def steps_to_owner(quad):
        owner = lax.rem(z_lo + quad // 2, 2) * 2 + lax.rem(bit + quad % 2, 2)
        return lax.rem(z_hi - owner + 4, 4)

    to_down, to_up = at(dz=-1), at(dz=1)

    def z_copy(kind):
        return pltpu.make_async_remote_copy(
            src_ref=zs.at[kind],
            dst_ref=zr.at[kind],
            send_sem=z_send.at[kind],
            recv_sem=z_recv.at[kind],
            device_id=(to_down, to_up)[kind % 2],
            device_id_type=MESH,
        )

    def direct_copy(steps, r):
        i, start = STRAIGHT[r]
        rows = pl.ds(start, RUNS[r][1])
        return pltpu.make_async_remote_copy(
            src_ref=ds.at[steps - 1, :, rows],
            dst_ref=dr.at[steps - 1, :, rows],
            send_sem=d_send.at[steps - 1, i],
            recv_sem=d_recv.at[steps - 1, i],
            device_id=at(dz=-steps),
            device_id_type=MESH,
        )

    def collect(quad, r):
        start, count = RUNS[r]
        rows = pl.ds(start, count)
        for side in (0, 1):
            x_copy(quad, r, side, 1).wait_recv()
            x_copy(quad, r, side, 2).wait_recv()
        got = lambda side, kind: xr[quad, side, kind, :, rows].astype(F32)
        upper = keep[quad, 0:16, rows] + (got(0, 2) + got(1, 1))
        lower = keep[quad, 16:32, rows] + (got(0, 1) + got(1, 2))
        steps = steps_to_owner(quad)

        @pl.when(steps == 0)
        def _():
            own[0:16, rows] = upper
            own[16:32, rows] = lower

        if r != RELAYED:

            @pl.when(steps != 0)
            def _():
                ds[steps - 1, 0:16, pl.ds(STRAIGHT[r][1], count)] = upper.astype(BF16)
                ds[steps - 1, 16:32, pl.ds(STRAIGHT[r][1], count)] = lower.astype(BF16)
                direct_copy(steps, r).start()

            return

        @pl.when(steps == 2)
        def _():
            zs[0] = upper.astype(BF16)
            zs[1] = lower.astype(BF16)
            z_copy(0).start()
            z_copy(1).start()

        @pl.when(steps == 1)
        def _():
            zs[2] = lower.astype(BF16)
            z_copy(2).start()
            zkeep[0] = upper

        @pl.when(steps == 3)
        def _():
            zs[3] = upper.astype(BF16)
            z_copy(3).start()
            zkeep[1] = lower

    def z_relay():
        for side in (0, 1):
            z_copy(side).wait_recv()
            zs[4 + side] = (zkeep[side] + zr[side].astype(F32)).astype(BF16)
            z_copy(4 + side).start()

    def finish(r, scale):
        start, count = RUNS[r]
        rows = pl.ds(start, count)
        if r == RELAYED:
            for kind in (2, 3, 4, 5):
                z_copy(kind).wait_recv()
            upper = own[0:16, rows] + (zr[4].astype(F32) + zr[3].astype(F32))
            lower = own[16:32, rows] + (zr[2].astype(F32) + zr[5].astype(F32))
        else:
            for steps in (1, 2, 3):
                direct_copy(steps, r).wait_recv()
            parts = dr[:, :, pl.ds(STRAIGHT[r][1], count)].astype(F32)
            total = own[:, rows] + (parts[0] + parts[1] + parts[2])
            upper, lower = total[0:16], total[16:32]
        for k in range(count // 256):
            i = start // 256 + k
            columns = slice(k * 256, (k + 1) * 256)
            out[0:16, i * 256 : (i + 1) * 256] = upper[:, columns] * scale[i : i + 1, :]
            out[16:32, i * 256 : (i + 1) * 256] = lower[:, columns] * scale[i : i + 1, :]

    def partner(step):
        pair = lambda i: i + 1 - 2 * lax.rem(i, 2)
        if step < 2:
            return {"ex": ex, "feat": z_hi * 4 + (pair(x) if step == 0 else 3 - x)}
        return {"ex": ex, "feat": (pair(z_hi) if step == 2 else 3 - z_hi) * 4 + x}

    def self_copy(step):
        return pltpu.make_async_remote_copy(
            src_ref=sb.at[step],
            dst_ref=sr.at[step],
            send_sem=s_send.at[step],
            recv_sem=s_recv.at[step],
            device_id=partner(step),
            device_id_type=MESH,
        )

    def self_step(step):
        self_copy(step).wait_recv()
        sb[step + 1] = sb[step] + sr[step]
        if step < 3:
            self_copy(step + 1).start()

    mine = lax.rem(y - x + 8, 4) * 32 + core * BLOCK
    pre[0, pl.ds(pl.multiple_of(mine, BLOCK), BLOCK), :] = (query[...].astype(F32) * inverse).astype(BF16)

    ones = jnp.ones((8, 128), F32)

    def self_influence(r):
        start, count = RUNS[r]
        loads[r].wait()
        wide = train[pl.ds(start, count), :].astype(F32)
        squares = wide * wide * inverse
        part = squares[:, 0:128]
        for k in range(1, DEPTH // 128):
            part = part + squares[:, k * 128 : (k + 1) * 128]
        sums = lax.dot_general(ones, part, NT, preferred_element_type=F32, precision=lax.Precision.HIGHEST)
        for k in range(count // 256):
            sb[0, pl.ds(start // 256 + k, 1), :] = sums[0:1, k * 256 : (k + 1) * 256]

    pl.semaphore_wait(barrier, len(near))
    here = (0, 0, 0)
    send_block(here, (0, 1, 0), at(dy=-1))
    send_block(here, (0, 2, 0), at(dy=1))
    send_block(here, (0, 3, 0), at(dy=-2))
    send_block(here, (0, 0, 1), at(other_core=1))
    self_influence(0)
    send_block(here, (2, 0, 0), at(other_z=1))
    send_block(here, (1, 3, 0), at(dy=2))
    self_influence(1)
    self_influence(2)
    self_copy(0).start()

    for place in (1, 2, 3):
        forward(0, place)
    multiply_half(0)
    for place in (0, 1, 2, 3):
        wait_block(0, place, 1)
    multiply_half(1)
    forward(2, 0)
    multiply(0, 1)
    forward(1, 3)
    multiply(0, 2)
    for place in (1, 2, 3):
        forward(2, place)
    self_step(0)
    for place in (0, 1, 2, 3):
        wait_block(2, place, 1)
    multiply(2, 0)
    for place in (2, 1, 0):
        forward(1, place)
    relay(0, 0)
    multiply(2, 1)
    relay(0, 1)
    multiply(2, 2)
    for place in (0, 1, 2, 3):
        wait_block(1, place, 1)
    multiply(1, 0)
    relay(0, 2)
    self_step(1)
    relay(2, 0)
    for place in (3, 2, 1, 0):
        forward(3, place)
    collect(0, 0)
    relay(2, 1)
    relay(2, 2)
    for place in (0, 1, 2, 3):
        wait_block(3, place, 1)
    multiply(3, 0)
    multiply(1, 1)
    collect(0, 1)
    collect(0, 2)
    relay(1, 0)
    multiply(3, 1)
    multiply(1, 2)
    multiply(3, 2)
    collect(2, 0)
    relay(3, 0)
    relay(1, 1)
    self_step(2)
    collect(2, 1)
    collect(2, 2)
    relay(3, 1)
    collect(1, 0)
    relay(1, 2)
    relay(3, 2)
    collect(3, 0)
    self_step(3)
    scale = lax.rsqrt(sb[4] + EPSILON)
    collect(1, 1)
    collect(3, 1)
    collect(1, 2)
    collect(3, 2)
    z_relay()
    finish(0, scale)
    finish(1, scale)
    finish(2, scale)

    for copy in sent:
        copy.wait_send()
    for quad in range(4):
        for r in range(len(RUNS)):
            for side in (0, 1):
                for kind in range(3):
                    x_copy(quad, r, side, kind).wait_send()
    for kind in range(6):
        z_copy(kind).wait_send()
    for steps in (1, 2, 3):
        for r in STRAIGHT:
            direct_copy(steps, r).wait_send()
    for step in range(4):
        self_copy(step).wait_send()


def on_device(train_grads, query_grads, eigenvalues):
    dma = pltpu.SemaphoreType.DMA
    scores = pl.pallas_call(
        kernel,
        out_shape=pltpu.VMEM((OWNED, ROWS), F32),
        in_specs=[pl.BlockSpec(memory_space=pltpu.HBM)] * 3,
        out_specs=pl.BlockSpec(memory_space=pltpu.VMEM),
        scratch_shapes=[
            pltpu.VMEM((ROWS, DEPTH), BF16),
            pltpu.VMEM((BLOCK, DEPTH), BF16),
            pltpu.VMEM((1, DEPTH), F32),
            pltpu.VMEM((4, 128, DEPTH), BF16),
            pltpu.VMEM((4, 64, ROWS), F32),
            pltpu.VMEM((4, 2, 3, 16, ROWS), BF16),
            pltpu.VMEM((4, 2, 3, 16, ROWS), BF16),
            pltpu.VMEM((6, 16, LONG), BF16),
            pltpu.VMEM((6, 16, LONG), BF16),
            pltpu.VMEM((2, 16, LONG), F32),
            pltpu.VMEM((3, OWNED, ROWS - LONG), BF16),
            pltpu.VMEM((3, OWNED, ROWS - LONG), BF16),
            pltpu.VMEM((OWNED, ROWS), F32),
            pltpu.VMEM((5, 8, 256), F32),
            pltpu.VMEM((4, 8, 256), F32),
            dma((len(RUNS) + 2,)),
            dma((32,)),
            dma((32,)),
            dma((4 * len(RUNS), 2, 3)),
            dma((4 * len(RUNS), 2, 3)),
            dma((6,)),
            dma((6,)),
            dma((3, len(STRAIGHT))),
            dma((3, len(STRAIGHT))),
            dma((4,)),
            dma((4,)),
        ],
        compiler_params=pltpu.CompilerParams(
            collective_id=0, has_side_effects=True, vmem_limit_bytes=60 * 2**20
        ),
        cost_estimate=pl.CostEstimate(flops=2 * ROWS * DEPTH * 512, bytes_accessed=6 * 2**20, transcendentals=0),
    )(train_grads, query_grads, eigenvalues.reshape(1, DEPTH))
    return scores.T


def solution(mesh):
    placed = (P("ex", "feat"), P("ex", "feat"), P("feat"))
    return jax.shard_map(
        on_device, mesh=mesh, in_specs=placed, out_specs=P("ex", "feat"), check_vma=False
    )
```
